32 devices in a mesh: dom: 2 (over x), tx: 2 (over core), cell: 8 (over z, y).
Axes of the slice: x: 2, y: 2, z: 4, core: 2. Of those that a mesh axis runs over, the one named last changes fastest.
Arguments:
- sensitivity: bfloat16 [4096, 16384], P(('dom', 'tx'), 'cell'), parts along dimension 0, may hold values from -0.25 to 0.25
- cell_weight: float32 [32768], P(('dom', 'cell')), parts along dimension 0, may hold values from 0.05 to 1
- pair_mask: int32 [16, 8], P('dom'), parts along dimension 0, may hold values from 0 to 1, as said below
- level_index: int32 [16], P('dom'), parts along dimension 0, may hold values from 0 to 3
- damp_levels: float32 [8], P('dom'), parts along dimension 0, may hold values from 0.5 to 8
Outputs:
- gram: float32 [4096, 2048], P(('dom', 'cell'), 'tx'), parts along dimension 0
The draws below stay inside these ranges and needn't reach their ends.
There are 2 independent parts, one for each index of `dom`. The reference program is written for one: setup_inputs(seed, part) draws one part's arguments, and reference() takes and returns one part's arrays. A program takes and returns all parts, laid end to end along the dimension named above; each array names one. Nothing has to cross between parts.
Inputs may be any that keep to these rules, and one draw needn't show every extreme that they name: `pair_mask`: symmetric, with ones on the diagonal.
All inputs are finite; a program needn't handle non-finite values.
Results may differ from the reference program's by a relative error of at most 0.00085.
Values may be sent and summed in bfloat16 or wider, within the bound.
A program may use at most 64 MiB of HBM per device.

```python
import math
import jax
import jax.numpy as jnp
from jax import lax

NBLK = 8
BLK_ROWS = 256
LEVELS = 4
ROWS = 2048
CELLS = 16384


def draw_pair_mask(key, part):
    key = jax.random.fold_in(key, 11)
    coins = jax.random.randint(key, (NBLK, NBLK), 0, 2).astype(jnp.int32)
    upper = jnp.triu(coins, 1)
    return (upper + upper.T + jnp.eye(NBLK, dtype=jnp.int32)).astype(jnp.int32)


def with_ends(array, own_key, low, high):
    shape = array.shape
    place = [jax.random.randint(jax.random.fold_in(own_key, axis), (), 0, shape[axis]) for axis in range(len(shape))]
    array = array.at[tuple(place)].set(low)
    longest = shape.index(max(shape))
    place[longest] = (place[longest] + 1) % shape[longest]
    return array.at[tuple(place)].set(high)


def spiked(array, stream_key, source, target, shards_of, factor):
    def block_of(axis_at):
        return (jnp.arange(array.shape[axis_at]) // (array.shape[axis_at] // shards_of)).reshape((-1,) + (1,) * (array.ndim - 1 - axis_at))

    first = jax.random.permutation(stream_key, shards_of)[block_of(target)]
    other_side = (block_of(target) + shards_of // 2) % shards_of
    return jnp.where((block_of(source) == first) | (block_of(source) == other_side), factor * array, array)


def block_scale(rng, dims, split, smallest, high):
    def one(dim, blocks):
        heights = jax.random.uniform(jax.random.fold_in(jax.random.fold_in(rng, 6), dim), (blocks,), jnp.float32, smallest / len(split), high / len(split))
        return jnp.repeat(jnp.exp(heights), dims[dim] // blocks).reshape((-1,) + (1,) * (len(dims) - dim - 1))

    loudness = one(*split[0])
    for cut in split[1:]:
        loudness = loudness * one(*cut)
    return loudness


def noise_with(own_key, shape, width, most, shards, heavy, kind=jnp.bfloat16):
    array = width * jax.random.normal(own_key, shape, jnp.float32)
    if shards:
        array = array * block_scale(own_key, shape, shards, -0.22, 0.18)
    return jnp.clip(spiked(array, jax.random.fold_in(own_key, 3), *heavy), -most, most).astype(kind)


def setup_inputs(seed: int = 0, part: int = 0) -> dict:
    keys = jax.random.split(jax.random.key(seed), 6)
    own_keys = jax.random.split(jax.random.fold_in(keys[5], part), 6)
    sensitivity = noise_with(own_keys[0], (ROWS, CELLS), (CELLS // 16) ** -0.5, 0.25, ((0, 2), (1, 8)), (1, 0, 8, 2.0))
    cell_weight = jnp.clip(jnp.exp(math.log(1.0) - 2.9957323 * jax.random.uniform(own_keys[1], (CELLS,), jnp.float32) ** block_scale(own_keys[1], (CELLS,), ((0, 8),), -0.2, 0.2)), 0.05, 1.0)
    pair_mask = draw_pair_mask(jax.random.fold_in(jax.random.fold_in(keys[5], part), 71), part)
    level_index = with_ends(jax.random.randint(own_keys[3], (NBLK,), 0, LEVELS), jax.random.fold_in(own_keys[3], 1), 0, LEVELS - 1).astype(jnp.int32)
    damp_levels = jnp.clip(jnp.exp(jax.random.uniform(own_keys[4], (LEVELS,), jnp.float32, math.log(0.5), math.log(8.0))), 0.5, 8.0)
    return {"sensitivity": sensitivity, "cell_weight": cell_weight, "pair_mask": pair_mask, "level_index": level_index, "damp_levels": damp_levels}


def reference(sensitivity, cell_weight, pair_mask, level_index, damp_levels):
    weighted = (sensitivity.astype(jnp.float32) * cell_weight[None, :]).astype(jnp.bfloat16)
    products = lax.dot_general(sensitivity, weighted, (((1,), (1,)), ((), ())), preferred_element_type=jnp.float32)
    group_ids = (jnp.arange(ROWS) // BLK_ROWS).astype(jnp.int32)
    mask_full = pair_mask[group_ids][:, group_ids].astype(jnp.float32)
    damping = damp_levels[level_index][group_ids]
    return products * mask_full + jnp.diag(damping)
```

```python
import functools

import jax
import jax.numpy as jnp
from jax import lax
from jax.experimental import pallas as pl
from jax.experimental.pallas import tpu as pltpu
from jax.sharding import PartitionSpec as P

MESH = pl.DeviceIdType.MESH
WIRE = jnp.int16
TOP = 32752.0
HEAD = 16


def contract(left, right):
    return lax.dot_general(
        left, right, (((1,), (1,)), ((), ())), preferred_element_type=jnp.float32
    )


def write(ref, value):
    side = value.shape[0]
    peak = jnp.maximum(jnp.max(jnp.abs(value), axis=0, keepdims=True), 2.0**-60)
    power = jnp.ceil(jnp.log2(peak))
    ref[pl.ds(0, side), :] = jnp.round(value * (jnp.exp2(-power) * TOP)).astype(jnp.int32).astype(WIRE)
    head = jnp.broadcast_to(power.astype(jnp.int32), (HEAD, value.shape[1]))
    ref[pl.ds(side, HEAD), :] = head.astype(WIRE)


def read(ref):
    side = ref.shape[0] - HEAD
    power = ref[pl.ds(side, HEAD), :].astype(jnp.int32).astype(jnp.float32)[:1, :]
    whole = ref[pl.ds(0, side), :].astype(jnp.int32).astype(jnp.float32)
    return whole * (jnp.exp2(power) * (1.0 / TOP))


def gram_kernel(
    side, w_ref, s_ref, out_ref,
    sall, wgt, ysend, yrecv, zsend, zrecv, acc, msend, mrecv,
    load_sem, gsend_sem, grecv_sem, ysend_sem, yrecv_sem, zsend_sem, zrecv_sem, msend_sem, mrecv_sem,
):
    t = lax.axis_index("tx")
    c = lax.axis_index("cell")
    z, y = c // 2, c % 2

    def block(r):
        return pl.ds(pl.multiple_of(r * side, side), side)

    def load(i):
        return pltpu.make_async_copy(
            s_ref.at[pl.ds(i * side, side), :], sall.at[0, pl.ds(i * side, side), :], load_sem.at[i]
        )

    for i in range(4):
        load(i).start()

    barrier = pltpu.get_barrier_semaphore()
    for k in range(1, 16):
        pl.semaphore_signal(
            barrier, inc=1,
            device_id={"tx": (t + k // 8) % 2, "cell": (c + k % 8) % 8},
            device_id_type=MESH,
        )

    def gather(r):
        return pltpu.make_async_remote_copy(
            src_ref=s_ref.at[block(r), :], dst_ref=sall.at[1, block(r), :],
            send_sem=gsend_sem.at[r], recv_sem=grecv_sem.at[r],
            device_id={"tx": 1 - t}, device_id_type=MESH,
        )

    pl.semaphore_wait(barrier, 15)
    for r in ((1 - y) + 2, 1 - y, y + 2, y):
        gather(r).start()

    for i in range(4):
        load(i).wait()
        rows = pl.ds(i * side, side)
        wgt[rows, :] = (sall[0, rows, :].astype(jnp.float32) * w_ref[...]).astype(jnp.bfloat16)

    def place(i, a):
        r = a + 2 * (i % 2)
        e = i // 2
        half = (r + e) // 4
        return r, (r + e) % 4, half, r + e == 4

    def product(i, a):
        r, q, half, first = place(i, a)

        @pl.when(first)
        def _():
            gather(r).wait_recv()

        return contract(sall[half, block(r), :], wgt[block(q), :])

    def ycopy(i):
        return pltpu.make_async_remote_copy(
            src_ref=ysend.at[i], dst_ref=yrecv.at[i],
            send_sem=ysend_sem.at[i], recv_sem=yrecv_sem.at[i],
            device_id={"cell": 2 * z + 1 - y}, device_id_type=MESH,
        )

    def zcopy(i, q, owner, source):
        return pltpu.make_async_remote_copy(
            src_ref=zsend.at[i], dst_ref=zrecv.at[source, q],
            send_sem=zsend_sem.at[i], recv_sem=zrecv_sem.at[source, q],
            device_id={"cell": 2 * owner + y}, device_id_type=MESH,
        )

    def mcopy(q, slot):
        return pltpu.make_async_remote_copy(
            src_ref=msend.at[q], dst_ref=mrecv.at[slot],
            send_sem=msend_sem.at[q], recv_sem=mrecv_sem.at[slot],
            device_id={"cell": 4 * t + q, "tx": c // 4}, device_id_type=MESH,
        )

    def first_phase(i, carry):
        write(ysend.at[i], product(i, 1 - y))
        ycopy(i).start()
        return carry

    lax.fori_loop(0, 10, first_phase, 0)

    def owner_of(i):
        r, q, half, _ = place(i, y)
        return q, 2 * ((t + half) % 2) + r // 2

    def second_phase(i, carry):
        q, owner = owner_of(i)
        part = product(i, y)
        ycopy(i).wait_recv()
        part = part + read(yrecv.at[i])

        @pl.when(owner == z)
        def _():
            acc[q] = part

        @pl.when(owner != z)
        def _():
            write(zsend.at[i], part)
            zcopy(i, q, owner, z).start()

        return carry

    lax.fori_loop(0, 10, second_phase, 0)

    rank = c % 4
    same = c // 4 == t

    def held(q):
        return jnp.where(same, q >= rank, q <= rank)

    for q in range(4):
        columns = pl.ds(q * side, side)

        @pl.when(held(q))
        def _():
            total = acc[q]
            for k in range(1, 4):
                source = (z + k) % 4
                zcopy(0, q, z, source).wait_recv()
                total = total + read(zrecv.at[source, q])
            out_ref[:, columns] = total

            @pl.when(q != rank)
            def _():
                write(msend.at[q], total)
                mcopy(q, rank).start()

    for q in range(4):
        columns = pl.ds(q * side, side)

        @pl.when(jnp.logical_not(held(q)))
        def _():
            mcopy(q, q).wait_recv()
            out_ref[:, columns] = read(mrecv.at[q]).T

    for r in range(4):
        gather(r).wait_send()

    def drain(i, carry):
        ycopy(i).wait_send()
        q, owner = owner_of(i)

        @pl.when(owner != z)
        def _():
            zcopy(i, q, owner, z).wait_send()

        return carry

    lax.fori_loop(0, 10, drain, 0)
    for q in range(4):
        @pl.when(jnp.logical_and(held(q), q != rank))
        def _():
            mcopy(q, rank).wait_send()


def gram_sums(sensitivity, cell_weight, groups):
    own_rows, cells = sensitivity.shape
    side = 2 * own_rows // groups
    tile = (side, side)
    wire = (side + HEAD, side)
    dma = pltpu.SemaphoreType.DMA
    return pl.pallas_call(
        functools.partial(gram_kernel, side),
        out_shape=jax.ShapeDtypeStruct((side, own_rows), jnp.float32),
        in_specs=[
            pl.BlockSpec(memory_space=pltpu.VMEM),
            pl.BlockSpec(memory_space=pl.ANY),
        ],
        out_specs=pl.BlockSpec(memory_space=pltpu.VMEM),
        scratch_shapes=[
            pltpu.VMEM((2, own_rows, cells), jnp.bfloat16),
            pltpu.VMEM((own_rows, cells), jnp.bfloat16),
            pltpu.VMEM((10,) + wire, WIRE),
            pltpu.VMEM((10,) + wire, WIRE),
            pltpu.VMEM((10,) + wire, WIRE),
            pltpu.VMEM((4, 4) + wire, WIRE),
            pltpu.VMEM((4,) + tile, jnp.float32),
            pltpu.VMEM((4,) + wire, WIRE),
            pltpu.VMEM((4,) + wire, WIRE),
            dma((4,)), dma((4,)), dma((4,)),
            dma((10,)), dma((10,)), dma((10,)), dma((4, 4)), dma((4,)), dma((4,)),
        ],
        compiler_params=pltpu.CompilerParams(
            collective_id=0, has_side_effects=True, vmem_limit_bytes=48 * 1024 * 1024
        ),
        cost_estimate=pl.CostEstimate(
            flops=2 * 20 * side * side * cells, bytes_accessed=own_rows * cells * 2, transcendentals=0
        ),
    )(cell_weight[None, :], sensitivity)


def plain_sums(sensitivity, cell_weight):
    weighted = (sensitivity.astype(jnp.float32) * cell_weight[None, :]).astype(jnp.bfloat16)
    everyone = lax.all_gather(sensitivity, "tx", axis=0, tiled=True)
    return lax.psum_scatter(contract(everyone, weighted), "cell", scatter_dimension=0, tiled=True)


def local(sensitivity, cell_weight, pair_mask, level_index, damp_levels):
    own_rows = sensitivity.shape[0]
    groups = pair_mask.shape[0]
    total_rows = own_rows * lax.axis_size("tx")
    part_rows = total_rows // lax.axis_size("cell")
    group_rows = total_rows // groups
    tx_pos = lax.axis_index("tx")
    cell_pos = lax.axis_index("cell")
    if lax.axis_size("tx") == 2 and lax.axis_size("cell") == 8 and groups == 8:
        summed = gram_sums(sensitivity, cell_weight, groups)
    else:
        summed = plain_sums(sensitivity, cell_weight)
    group = cell_pos * part_rows // group_rows
    col_groups = tx_pos * own_rows // group_rows + jnp.arange(own_rows // group_rows, dtype=jnp.int32)
    mask_row = pair_mask[group][col_groups].astype(jnp.float32)
    damp = damp_levels[level_index[group]]
    row_ids = cell_pos * part_rows + lax.broadcasted_iota(jnp.int32, summed.shape, 0)
    col_ids = tx_pos * own_rows + lax.broadcasted_iota(jnp.int32, summed.shape, 1)
    col_mask = jnp.repeat(mask_row, group_rows)[None, :]
    return summed * col_mask + jnp.where(row_ids == col_ids, damp, 0.0)


def solution(mesh):
    in_specs = (P(("dom", "tx"), "cell"), P(("dom", "cell")), P("dom", None), P("dom"), P("dom"))
    out_specs = P(("dom", "cell"), "tx")
    return jax.shard_map(local, mesh=mesh, in_specs=in_specs, out_specs=out_specs, check_vma=False)
```

```python
import functools

import jax
import jax.numpy as jnp
from jax import lax
from jax.experimental import pallas as pl
from jax.experimental.pallas import tpu as pltpu
from jax.sharding import PartitionSpec as P

MESH = pl.DeviceIdType.MESH
WIRE = jnp.int16
TOP = 32752.0
HEAD = 16


def contract(left, right):
    return lax.dot_general(
        left, right, (((1,), (1,)), ((), ())), preferred_element_type=jnp.float32
    )


def write(ref, value):
    side = value.shape[0]
    peak = jnp.maximum(jnp.max(jnp.abs(value), axis=0, keepdims=True), 2.0**-60)
    power = jnp.ceil(jnp.log2(peak))
    ref[pl.ds(0, side), :] = jnp.round(value * (jnp.exp2(-power) * TOP)).astype(jnp.int32).astype(WIRE)
    head = jnp.broadcast_to(power.astype(jnp.int32), (HEAD, value.shape[1]))
    ref[pl.ds(side, HEAD), :] = head.astype(WIRE)


def read(ref):
    side = ref.shape[0] - HEAD
    power = ref[pl.ds(side, HEAD), :].astype(jnp.int32).astype(jnp.float32)[:1, :]
    whole = ref[pl.ds(0, side), :].astype(jnp.int32).astype(jnp.float32)
    return whole * (jnp.exp2(power) * (1.0 / TOP))


def gram_kernel(
    side, w_ref, mask_ref, level_ref, damp_ref, s_ref, out_ref,
    sall, wgt, ysend, yrecv, zsend, zrecv, acc, msend, mrecv,
    load_sem, gsend_sem, grecv_sem, ysend_sem, yrecv_sem, zsend_sem, zrecv_sem, msend_sem, mrecv_sem,
):
    t = lax.axis_index("tx")
    c = lax.axis_index("cell")
    z, y = c // 2, c % 2

    def block(r):
        return pl.ds(pl.multiple_of(r * side, side), side)

    def load(i):
        return pltpu.make_async_copy(
            s_ref.at[pl.ds(i * side, side), :], sall.at[0, pl.ds(i * side, side), :], load_sem.at[i]
        )

    for i in range(4):
        load(i).start()

    barrier = pltpu.get_barrier_semaphore()
    for k in range(1, 16):
        pl.semaphore_signal(
            barrier, inc=1,
            device_id={"tx": (t + k // 8) % 2, "cell": (c + k % 8) % 8},
            device_id_type=MESH,
        )

    def gather(r):
        return pltpu.make_async_remote_copy(
            src_ref=s_ref.at[block(r), :], dst_ref=sall.at[1, block(r), :],
            send_sem=gsend_sem.at[r], recv_sem=grecv_sem.at[r],
            device_id={"tx": 1 - t}, device_id_type=MESH,
        )

    def weigh(i):
        load(i).wait()
        rows = pl.ds(i * side, side)
        wgt[rows, :] = (sall[0, rows, :].astype(jnp.float32) * w_ref[...]).astype(jnp.bfloat16)

    weigh(0)
    pl.semaphore_wait(barrier, 15)
    for r in ((1 - y) + 2, 1 - y, y + 2, y):
        gather(r).start()
    for i in range(1, 4):
        weigh(i)

    def place(i, a):
        r = a + 2 * (i % 2)
        e = i // 2
        half = (r + e) // 4
        return r, (r + e) % 4, half, r + e == 4

    def product(i, a):
        r, q, half, first = place(i, a)

        @pl.when(first)
        def _():
            gather(r).wait_recv()

        return contract(sall[half, block(r), :], wgt[block(q), :])

    def ycopy(i):
        return pltpu.make_async_remote_copy(
            src_ref=ysend.at[i], dst_ref=yrecv.at[i],
            send_sem=ysend_sem.at[i], recv_sem=yrecv_sem.at[i],
            device_id={"cell": 2 * z + 1 - y}, device_id_type=MESH,
        )

    def zcopy(i, q, owner, source):
        return pltpu.make_async_remote_copy(
            src_ref=zsend.at[i], dst_ref=zrecv.at[source, q],
            send_sem=zsend_sem.at[i], recv_sem=zrecv_sem.at[source, q],
            device_id={"cell": 2 * owner + y}, device_id_type=MESH,
        )

    def mcopy(q, slot):
        return pltpu.make_async_remote_copy(
            src_ref=msend.at[q], dst_ref=mrecv.at[slot],
            send_sem=msend_sem.at[q], recv_sem=mrecv_sem.at[slot],
            device_id={"cell": 4 * t + q, "tx": c // 4}, device_id_type=MESH,
        )

    def first_phase(i, carry):
        write(ysend.at[i], product(i, 1 - y))
        ycopy(i).start()
        return carry

    lax.fori_loop(0, 10, first_phase, 0)

    def owner_of(i):
        r, q, half, _ = place(i, y)
        return q, 2 * ((t + half) % 2) + r // 2

    def second_phase(i, carry):
        q, owner = owner_of(i)
        part = product(i, y)
        ycopy(i).wait_recv()
        part = part + read(yrecv.at[i])

        @pl.when(owner == z)
        def _():
            acc[q] = part

        @pl.when(owner != z)
        def _():
            write(zsend.at[i], part)
            zcopy(i, q, owner, z).start()

        return carry

    lax.fori_loop(0, 10, second_phase, 0)

    rank = c % 4
    same = c // 4 == t

    mask_row = mask_ref[pl.ds(c, 1), :].astype(jnp.float32)
    group_ids = lax.broadcasted_iota(jnp.int32, mask_row.shape, 1)
    level = jnp.sum(jnp.where(group_ids == c, level_ref[...], 0), axis=1, keepdims=True)
    level_ids = lax.broadcasted_iota(jnp.int32, damp_ref.shape, 1)
    damp = jnp.sum(jnp.where(level_ids == level, damp_ref[...], 0.0), axis=1, keepdims=True)

    def masked(q, total):
        mask = jnp.sum(jnp.where(group_ids == 4 * t + q, mask_row, 0.0), axis=1, keepdims=True)
        return total * mask

    def held(q):
        return jnp.where(same, q >= rank, q <= rank)

    for q in range(4):
        columns = pl.ds(q * side, side)

        @pl.when(held(q))
        def _():
            total = acc[q]
            for k in range(1, 4):
                source = (z + k) % 4
                zcopy(0, q, z, source).wait_recv()
                total = total + read(zrecv.at[source, q])
            out_ref[:, columns] = masked(q, total)

            @pl.when(jnp.logical_and(same, q == rank))
            def _():
                row_ids = lax.broadcasted_iota(jnp.int32, total.shape, 0)
                col_ids = lax.broadcasted_iota(jnp.int32, total.shape, 1)
                out_ref[:, columns] += jnp.where(row_ids == col_ids, damp, 0.0)

            @pl.when(q != rank)
            def _():
                write(msend.at[q], total)
                mcopy(q, rank).start()

    for q in range(4):
        columns = pl.ds(q * side, side)

        @pl.when(jnp.logical_not(held(q)))
        def _():
            mcopy(q, q).wait_recv()
            out_ref[:, columns] = masked(q, read(mrecv.at[q]).T)

    for r in range(4):
        gather(r).wait_send()

    def drain(i, carry):
        ycopy(i).wait_send()
        q, owner = owner_of(i)

        @pl.when(owner != z)
        def _():
            zcopy(i, q, owner, z).wait_send()

        return carry

    lax.fori_loop(0, 10, drain, 0)
    for q in range(4):
        @pl.when(jnp.logical_and(held(q), q != rank))
        def _():
            mcopy(q, rank).wait_send()


def gram_tiles(sensitivity, cell_weight, pair_mask, level_index, damp_levels):
    groups = pair_mask.shape[0]
    own_rows, cells = sensitivity.shape
    side = 2 * own_rows // groups
    tile = (side, side)
    wire = (side + HEAD, side)
    dma = pltpu.SemaphoreType.DMA
    return pl.pallas_call(
        functools.partial(gram_kernel, side),
        out_shape=jax.ShapeDtypeStruct((side, own_rows), jnp.float32),
        in_specs=[
            pl.BlockSpec(memory_space=pltpu.VMEM),
            pl.BlockSpec(memory_space=pltpu.VMEM),
            pl.BlockSpec(memory_space=pltpu.VMEM),
            pl.BlockSpec(memory_space=pltpu.VMEM),
            pl.BlockSpec(memory_space=pltpu.HBM),
        ],
        out_specs=pl.BlockSpec(memory_space=pltpu.VMEM),
        scratch_shapes=[
            pltpu.VMEM((2, own_rows, cells), jnp.bfloat16),
            pltpu.VMEM((own_rows, cells), jnp.bfloat16),
            pltpu.VMEM((10,) + wire, WIRE),
            pltpu.VMEM((10,) + wire, WIRE),
            pltpu.VMEM((10,) + wire, WIRE),
            pltpu.VMEM((4, 4) + wire, WIRE),
            pltpu.VMEM((4,) + tile, jnp.float32),
            pltpu.VMEM((4,) + wire, WIRE),
            pltpu.VMEM((4,) + wire, WIRE),
            dma((4,)), dma((4,)), dma((4,)),
            dma((10,)), dma((10,)), dma((10,)), dma((4, 4)), dma((4,)), dma((4,)),
        ],
        compiler_params=pltpu.CompilerParams(
            collective_id=0, has_side_effects=True, vmem_limit_bytes=60 * 1024 * 1024
        ),
        cost_estimate=pl.CostEstimate(
            flops=2 * 20 * side * side * cells, bytes_accessed=own_rows * cells * 2, transcendentals=0
        ),
    )(cell_weight[None, :], pair_mask, level_index[None, :], damp_levels[None, :], sensitivity)


def plain_sums(sensitivity, cell_weight):
    weighted = (sensitivity.astype(jnp.float32) * cell_weight[None, :]).astype(jnp.bfloat16)
    everyone = lax.all_gather(sensitivity, "tx", axis=0, tiled=True)
    return lax.psum_scatter(contract(everyone, weighted), "cell", scatter_dimension=0, tiled=True)


def local(sensitivity, cell_weight, pair_mask, level_index, damp_levels):
    own_rows = sensitivity.shape[0]
    groups = pair_mask.shape[0]
    total_rows = own_rows * lax.axis_size("tx")
    part_rows = total_rows // lax.axis_size("cell")
    group_rows = total_rows // groups
    tx_pos = lax.axis_index("tx")
    cell_pos = lax.axis_index("cell")
    if lax.axis_size("tx") == 2 and lax.axis_size("cell") == 8 and groups == 8:
        return gram_tiles(sensitivity, cell_weight, pair_mask, level_index, damp_levels)
    summed = plain_sums(sensitivity, cell_weight)
    group = cell_pos * part_rows // group_rows
    col_groups = tx_pos * own_rows // group_rows + jnp.arange(own_rows // group_rows, dtype=jnp.int32)
    mask_row = pair_mask[group][col_groups].astype(jnp.float32)
    damp = damp_levels[level_index[group]]
    row_ids = cell_pos * part_rows + lax.broadcasted_iota(jnp.int32, summed.shape, 0)
    col_ids = tx_pos * own_rows + lax.broadcasted_iota(jnp.int32, summed.shape, 1)
    col_mask = jnp.repeat(mask_row, group_rows)[None, :]
    return summed * col_mask + jnp.where(row_ids == col_ids, damp, 0.0)


def solution(mesh):
    in_specs = (P(("dom", "tx"), "cell"), P(("dom", "cell")), P("dom", None), P("dom"), P("dom"))
    out_specs = P(("dom", "cell"), "tx")
    return jax.shard_map(local, mesh=mesh, in_specs=in_specs, out_specs=out_specs, check_vma=False)
```

```python
import functools

import jax
import jax.numpy as jnp
from jax import lax
from jax.experimental import pallas as pl
from jax.experimental.pallas import tpu as pltpu
from jax.sharding import PartitionSpec as P

MESH = pl.DeviceIdType.MESH
WIRE = jnp.int16
TOP = 32752.0
HEAD = 16


def contract(left, right):
    return lax.dot_general(
        left, right, (((1,), (1,)), ((), ())), preferred_element_type=jnp.float32
    )


def write(ref, value):
    side = value.shape[0]
    peak = jnp.maximum(jnp.max(jnp.abs(value), axis=0, keepdims=True), 2.0**-60)
    power = jnp.ceil(jnp.log2(peak))
    ref[pl.ds(0, side), :] = jnp.round(value * (jnp.exp2(-power) * TOP)).astype(jnp.int32).astype(WIRE)
    head = jnp.broadcast_to(power.astype(jnp.int32), (HEAD, value.shape[1]))
    ref[pl.ds(side, HEAD), :] = head.astype(WIRE)


def read(ref):
    side = ref.shape[0] - HEAD
    power = ref[pl.ds(side, HEAD), :].astype(jnp.int32).astype(jnp.float32)[:1, :]
    whole = ref[pl.ds(0, side), :].astype(jnp.int32).astype(jnp.float32)
    return whole * (jnp.exp2(power) * (1.0 / TOP))


def gram_kernel(
    side, w_ref, mask_ref, level_ref, damp_ref, s_ref, out_ref,
    sall, wgt, ysend, yrecv, yhsend, yhrecv, zsend, zrecv, zhsend, zhrecv,
    acc, hacc, msend, mrecv, mhsend, mhrecv,
    load_sem, gsend_sem, grecv_sem, ysend_sem, yrecv_sem, zsend_sem, zrecv_sem, zhrecv_sem,
    msend_sem, mrecv_sem, mhsend_sem, mhrecv_sem,
):
    t = lax.axis_index("tx")
    c = lax.axis_index("cell")
    z, y = c // 2, c % 2
    rank = c % 4
    same = c // 4 == t
    half_side = side // 2

    def block(r):
        return pl.ds(pl.multiple_of(r * side, side), side)

    def load(i):
        return pltpu.make_async_copy(
            s_ref.at[pl.ds(i * side, side), :], sall.at[0, pl.ds(i * side, side), :], load_sem.at[i]
        )

    for i in (1, 2, 3, 0):
        load(i).start()

    barrier = pltpu.get_barrier_semaphore()
    for k in range(1, 16):
        pl.semaphore_signal(
            barrier, inc=1,
            device_id={"tx": (t + k // 8) % 2, "cell": (c + k % 8) % 8},
            device_id_type=MESH,
        )

    def gather(r):
        return pltpu.make_async_remote_copy(
            src_ref=s_ref.at[block(r), :], dst_ref=sall.at[1, block(r), :],
            send_sem=gsend_sem.at[r], recv_sem=grecv_sem.at[r],
            device_id={"tx": 1 - t}, device_id_type=MESH,
        )

    def weigh(i):
        rows = pl.ds(i * side, side)
        wgt[rows, :] = (sall[0, rows, :].astype(jnp.float32) * w_ref[...]).astype(jnp.bfloat16)

    def place(i, a):
        near = i < 4
        ri = jnp.where(near, i // 2, i % 2)
        e = jnp.where(near, 1 + i % 2, jnp.where(i < 6, 3, jnp.where(i < 8, 4, 0)))
        r = a + 2 * ri
        return r, e, (r + e) % 4, (r + e) // 4

    def product(i, a):
        r, e, q, half = place(i, a)

        @pl.when(r + e == 4)
        def _():
            gather(r).wait_recv()

        return contract(sall[half, block(r), :], wgt[block(q), :])

    def half_product(i, a, ref):
        r, e, q, half = place(i, a)

        @pl.when(r + e == 4)
        def _():
            gather(r).wait_recv()

        upper = (t + half) % 2
        for u in range(2):
            v = (u + upper) % 2
            rows = pl.ds(pl.multiple_of(r * side + u * half_side, half_side), half_side)
            cols = pl.ds(pl.multiple_of(q * side + v * half_side, half_side), half_side)
            ref[u * half_side:(u + 1) * half_side, :] = contract(sall[half, rows, :], wgt[cols, :])

    def ycopy(i, halved):
        src, dst = (yhsend.at[i - 6], yhrecv.at[i - 6]) if halved else (ysend.at[i], yrecv.at[i])
        return pltpu.make_async_remote_copy(
            src_ref=src, dst_ref=dst,
            send_sem=ysend_sem.at[i], recv_sem=yrecv_sem.at[i],
            device_id={"cell": 2 * z + 1 - y}, device_id_type=MESH,
        )

    def zcopy(i, q, owner, source, halved):
        src, dst = (zhsend.at[i - 6], zhrecv.at[source]) if halved else (zsend.at[i], zrecv.at[source, q])
        return pltpu.make_async_remote_copy(
            src_ref=src, dst_ref=dst,
            send_sem=zsend_sem.at[i], recv_sem=zhrecv_sem.at[source] if halved else zrecv_sem.at[source, q],
            device_id={"cell": 2 * owner + y}, device_id_type=MESH,
        )

    def mcopy(q, slot):
        return pltpu.make_async_remote_copy(
            src_ref=msend.at[q], dst_ref=mrecv.at[slot],
            send_sem=msend_sem.at[q], recv_sem=mrecv_sem.at[slot],
            device_id={"cell": 4 * t + q, "tx": c // 4}, device_id_type=MESH,
        )

    def mhcopy():
        return pltpu.make_async_remote_copy(
            src_ref=mhsend, dst_ref=mhrecv,
            send_sem=mhsend_sem.at[0], recv_sem=mhrecv_sem.at[0],
            device_id={"cell": 4 * t + rank, "tx": 1 - t}, device_id_type=MESH,
        )

    def send(i, carry):
        write(ysend.at[i], product(i, 1 - y))
        ycopy(i, False).start()
        return carry

    def send_half(i, carry):
        half_product(i, 1 - y, hacc.at[1])
        write(yhsend.at[i - 6], hacc[1])
        ycopy(i, True).start()
        return carry

    def owner_of(i):
        r, e, q, half = place(i, y)
        return q, 2 * ((t + half) % 2) + r // 2

    def keep(i, carry):
        q, owner = owner_of(i)
        part = product(i, y)
        ycopy(i, False).wait_recv()
        part = part + read(yrecv.at[i])

        @pl.when(owner == z)
        def _():
            acc[q] = part

        @pl.when(owner != z)
        def _():
            write(zsend.at[i], part)
            zcopy(i, q, owner, z, False).start()

        return carry

    def keep_half(i, carry):
        q, owner = owner_of(i)
        half_product(i, y, hacc.at[1])
        ycopy(i, True).wait_recv()
        part = hacc[1] + read(yhrecv.at[i - 6])

        @pl.when(owner == z)
        def _():
            hacc[0] = part

        @pl.when(owner != z)
        def _():
            write(zhsend.at[i - 6], part)
            zcopy(i, q, owner, z, True).start()

        return carry

    load(1).wait()
    weigh(1)
    load(2).wait()
    weigh(2)
    load(3).wait()
    load(0).wait()
    pl.semaphore_wait(barrier, 15)
    for r in ((1 - y) + 2, 1 - y, y + 2, y):
        gather(r).start()
    lax.fori_loop(0, 1, send, 0)
    weigh(3)
    lax.fori_loop(1, 2, send, 0)
    weigh(0)
    lax.fori_loop(2, 6, send, 0)
    lax.fori_loop(6, 8, send_half, 0)
    lax.fori_loop(8, 10, send, 0)

    mask_row = mask_ref[pl.ds(c, 1), :].astype(jnp.float32)
    group_ids = lax.broadcasted_iota(jnp.int32, mask_row.shape, 1)
    level = jnp.sum(jnp.where(group_ids == c, level_ref[...], 0), axis=1, keepdims=True)
    level_ids = lax.broadcasted_iota(jnp.int32, damp_ref.shape, 1)
    damp = jnp.sum(jnp.where(level_ids == level, damp_ref[...], 0.0), axis=1, keepdims=True)

    def masked(q, total):
        mask = jnp.sum(jnp.where(group_ids == 4 * t + q, mask_row, 0.0), axis=1, keepdims=True)
        return total * mask

    def distance(q):
        return (4 * t + q - c + 8) % 8

    def summed(q):
        total = acc[q]
        for k in range(1, 4):
            source = (z + k) % 4
            zcopy(0, q, z, source, False).wait_recv()
            total = total + read(zrecv.at[source, q])
        return total

    def mirrored(q):
        return jnp.logical_and(distance(q) >= 1, distance(q) <= 3)

    lax.fori_loop(0, 6, keep, 0)
    lax.fori_loop(6, 8, keep_half, 0)

    for q in range(4):
        @pl.when(mirrored(q))
        def _():
            total = summed(q)
            write(msend.at[q], total)
            mcopy(q, rank).start()
            out_ref[:, pl.ds(q * side, side)] = masked(q, total)

    def quarter(u, v):
        return (
            pl.ds(u * half_side, half_side) if isinstance(u, int)
            else pl.ds(pl.multiple_of(u * half_side, half_side), half_side),
            pl.ds(pl.multiple_of(rank * side + v * half_side, half_side), half_side),
        )

    @pl.when(jnp.logical_not(same))
    def _():
        total = hacc[0]
        for k in range(1, 4):
            source = (z + k) % 4
            zcopy(6, 0, z, source, True).wait_recv()
            total = total + read(zhrecv.at[source])
        write(mhsend, total)
        mhcopy().start()
        total = masked(rank, total)
        for u in range(2):
            rows, cols = quarter(u, (u + c // 4) % 2)
            out_ref[rows, cols] = total[u * half_side:(u + 1) * half_side, :]

    lax.fori_loop(8, 10, keep, 0)

    for q in range(4):
        @pl.when(distance(q) >= 5)
        def _():
            mcopy(q, q).wait_recv()
            out_ref[:, pl.ds(q * side, side)] = masked(q, read(mrecv.at[q]).T)

    @pl.when(jnp.logical_not(same))
    def _():
        mhcopy().wait_recv()
        total = masked(rank, read(mhrecv))
        for u in range(2):
            v = (u + 1 - c // 4) % 2
            rows, cols = quarter(v, u)
            out_ref[rows, cols] = total[u * half_side:(u + 1) * half_side, :].T

    @pl.when(same)
    def _():
        total = masked(rank, summed(rank))
        row_ids = lax.broadcasted_iota(jnp.int32, total.shape, 0)
        col_ids = lax.broadcasted_iota(jnp.int32, total.shape, 1)
        out_ref[:, block(rank)] = total + jnp.where(row_ids == col_ids, damp, 0.0)

    for r in range(4):
        gather(r).wait_send()

    def drain(halved, i, carry):
        ycopy(i, halved).wait_send()
        q, owner = owner_of(i)

        @pl.when(owner != z)
        def _():
            zcopy(i, q, owner, z, halved).wait_send()

        return carry

    lax.fori_loop(0, 6, functools.partial(drain, False), 0)
    lax.fori_loop(6, 8, functools.partial(drain, True), 0)
    lax.fori_loop(8, 10, functools.partial(drain, False), 0)
    for q in range(4):
        @pl.when(mirrored(q))
        def _():
            mcopy(q, rank).wait_send()

    @pl.when(jnp.logical_not(same))
    def _():
        mhcopy().wait_send()


def gram_tiles(sensitivity, cell_weight, pair_mask, level_index, damp_levels):
    groups = pair_mask.shape[0]
    own_rows, cells = sensitivity.shape
    side = 2 * own_rows // groups
    tile = (side, side)
    wire = (side + HEAD, side)
    slim = (side + HEAD, side // 2)
    dma = pltpu.SemaphoreType.DMA
    return pl.pallas_call(
        functools.partial(gram_kernel, side),
        out_shape=jax.ShapeDtypeStruct((side, own_rows), jnp.float32),
        in_specs=[
            pl.BlockSpec(memory_space=pltpu.VMEM),
            pl.BlockSpec(memory_space=pltpu.VMEM),
            pl.BlockSpec(memory_space=pltpu.VMEM),
            pl.BlockSpec(memory_space=pltpu.VMEM),
            pl.BlockSpec(memory_space=pltpu.HBM),
        ],
        out_specs=pl.BlockSpec(memory_space=pltpu.VMEM),
        scratch_shapes=[
            pltpu.VMEM((2, own_rows, cells), jnp.bfloat16),
            pltpu.VMEM((own_rows, cells), jnp.bfloat16),
            pltpu.VMEM((10,) + wire, WIRE),
            pltpu.VMEM((10,) + wire, WIRE),
            pltpu.VMEM((2,) + slim, WIRE),
            pltpu.VMEM((2,) + slim, WIRE),
            pltpu.VMEM((10,) + wire, WIRE),
            pltpu.VMEM((4, 4) + wire, WIRE),
            pltpu.VMEM((2,) + slim, WIRE),
            pltpu.VMEM((4,) + slim, WIRE),
            pltpu.VMEM((4,) + tile, jnp.float32),
            pltpu.VMEM((2, side, side // 2), jnp.float32),
            pltpu.VMEM((4,) + wire, WIRE),
            pltpu.VMEM((4,) + wire, WIRE),
            pltpu.VMEM(slim, WIRE),
            pltpu.VMEM(slim, WIRE),
            dma((4,)), dma((4,)), dma((4,)),
            dma((10,)), dma((10,)), dma((10,)), dma((4, 4)), dma((4,)),
            dma((4,)), dma((4,)), dma((1,)), dma((1,)),
        ],
        compiler_params=pltpu.CompilerParams(
            collective_id=0, has_side_effects=True, vmem_limit_bytes=60 * 1024 * 1024
        ),
        cost_estimate=pl.CostEstimate(
            flops=2 * 20 * side * side * cells, bytes_accessed=own_rows * cells * 2, transcendentals=0
        ),
    )(cell_weight[None, :], pair_mask, level_index[None, :], damp_levels[None, :], sensitivity)


def plain_sums(sensitivity, cell_weight):
    weighted = (sensitivity.astype(jnp.float32) * cell_weight[None, :]).astype(jnp.bfloat16)
    everyone = lax.all_gather(sensitivity, "tx", axis=0, tiled=True)
    return lax.psum_scatter(contract(everyone, weighted), "cell", scatter_dimension=0, tiled=True)


def local(sensitivity, cell_weight, pair_mask, level_index, damp_levels):
    own_rows = sensitivity.shape[0]
    groups = pair_mask.shape[0]
    total_rows = own_rows * lax.axis_size("tx")
    part_rows = total_rows // lax.axis_size("cell")
    group_rows = total_rows // groups
    tx_pos = lax.axis_index("tx")
    cell_pos = lax.axis_index("cell")
    if lax.axis_size("tx") == 2 and lax.axis_size("cell") == 8 and groups == 8:
        return gram_tiles(sensitivity, cell_weight, pair_mask, level_index, damp_levels)
    summed = plain_sums(sensitivity, cell_weight)
    group = cell_pos * part_rows // group_rows
    col_groups = tx_pos * own_rows // group_rows + jnp.arange(own_rows // group_rows, dtype=jnp.int32)
    mask_row = pair_mask[group][col_groups].astype(jnp.float32)
    damp = damp_levels[level_index[group]]
    row_ids = cell_pos * part_rows + lax.broadcasted_iota(jnp.int32, summed.shape, 0)
    col_ids = tx_pos * own_rows + lax.broadcasted_iota(jnp.int32, summed.shape, 1)
    col_mask = jnp.repeat(mask_row, group_rows)[None, :]
    return summed * col_mask + jnp.where(row_ids == col_ids, damp, 0.0)


def solution(mesh):
    in_specs = (P(("dom", "tx"), "cell"), P(("dom", "cell")), P("dom", None), P("dom"), P("dom"))
    out_specs = P(("dom", "cell"), "tx")
    return jax.shard_map(local, mesh=mesh, in_specs=in_specs, out_specs=out_specs, check_vma=False)
```

```python
import functools

import jax
import jax.numpy as jnp
from jax import lax
from jax.experimental import pallas as pl
from jax.experimental.pallas import tpu as pltpu
from jax.sharding import PartitionSpec as P

MESH = pl.DeviceIdType.MESH
WIRE = jnp.int16
TOP = 32752.0
HEAD = 16
DISTANCES = (1, 2, 3, 4, 0)


def contract(left, right):
    return lax.dot_general(
        left, right, (((1,), (1,)), ((), ())), preferred_element_type=jnp.float32
    )


def write(ref, value):
    side = value.shape[0]
    peak = jnp.maximum(jnp.max(jnp.abs(value), axis=0, keepdims=True), 2.0**-60)
    power = jnp.ceil(jnp.log2(peak))
    ref[pl.ds(0, side), :] = jnp.round(value * (jnp.exp2(-power) * TOP)).astype(jnp.int32).astype(WIRE)
    head = jnp.broadcast_to(power.astype(jnp.int32), (HEAD, value.shape[1]))
    ref[pl.ds(side, HEAD), :] = head.astype(WIRE)


def read(ref):
    side = ref.shape[0] - HEAD
    power = ref[pl.ds(side, HEAD), :].astype(jnp.int32).astype(jnp.float32)[:1, :]
    whole = ref[pl.ds(0, side), :].astype(jnp.int32).astype(jnp.float32)
    return whole * (jnp.exp2(power) * (1.0 / TOP))


def gram_kernel(side, w_ref, mask_ref, level_ref, damp_ref, s_ref, out_ref, sall, wgt, *refs):
    ysend, yrecv, near_send, near_recv, far_send, far_recv, acc, msend, mrecv = (
        refs[n * 5:n * 5 + 5] for n in range(9)
    )
    (load_sem, gsend_sem, grecv_sem, ysend_sem, yrecv_sem, near_send_sem, near_recv_sem,
     far_send_sem, far_recv_sem, msend_sem, mrecv_sem) = refs[45:]
    t = lax.axis_index("tx")
    c = lax.axis_index("cell")
    z, y = c // 2, c % 2
    rank, upper, zb = c % 4, c // 4, z % 2
    half_side = side // 2

    def block(r):
        return pl.ds(pl.multiple_of(r * side, side), side)

    def load(i):
        return pltpu.make_async_copy(
            s_ref.at[pl.ds(i * side, side), :], sall.at[0, pl.ds(i * side, side), :], load_sem.at[i]
        )

    for i in range(4):
        load(i).start()

    barrier = pltpu.get_barrier_semaphore()
    for k in range(1, 16):
        pl.semaphore_signal(
            barrier, inc=1,
            device_id={"tx": (t + k // 8) % 2, "cell": (c + k % 8) % 8},
            device_id_type=MESH,
        )

    def remote(src, dst, send_sem, recv_sem, device):
        return pltpu.make_async_remote_copy(
            src_ref=src, dst_ref=dst, send_sem=send_sem, recv_sem=recv_sem,
            device_id=device, device_id_type=MESH,
        )

    def gather(r):
        return remote(
            s_ref.at[block(r), :], sall.at[1, block(r), :], gsend_sem.at[r], grecv_sem.at[r], {"tx": 1 - t}
        )

    def ycopy(k, s):
        return remote(
            ysend[k].at[s], yrecv[k].at[s], ysend_sem.at[2 * k + s], yrecv_sem.at[2 * k + s],
            {"cell": 2 * z + 1 - y},
        )

    def near_copy(k):
        return remote(
            near_send[k], near_recv[k], near_send_sem.at[k], near_recv_sem.at[k],
            {"cell": 2 * (z + 1 - 2 * zb) + y},
        )

    def far_copy(k):
        return remote(
            far_send[k], far_recv[k], far_send_sem.at[k], far_recv_sem.at[k], {"cell": (c + 4) % 8}
        )

    def mcopy(k):
        return remote(
            msend[k], mrecv[k], msend_sem.at[k], mrecv_sem.at[k],
            {"cell": (c + DISTANCES[k]) % 8, "tx": upper},
        )

    def weigh(i):
        rows = block(i)
        wgt[rows, :] = (sall[0, rows, :].astype(jnp.float32) * w_ref[...]).astype(jnp.bfloat16)

    def product(e, r):
        half, q = (r + e) // 4, (r + e) % 4
        if e:
            @pl.when(r + e == 4)
            def _():
                gather(r).wait_recv()
        if e != 4:
            return contract(sall[half, block(r), :], wgt[block(q), :])
        quarters = []
        for u in range(2):
            v = (u + t + half) % 2
            rows = pl.ds(pl.multiple_of(r * side + u * half_side, half_side), half_side)
            cols = pl.ds(pl.multiple_of(q * side + v * half_side, half_side), half_side)
            quarters.append(contract(sall[half, rows, :], wgt[cols, :]))
        return jnp.concatenate(quarters, axis=0)

    for i in range(4):
        load(i).wait()
    first = 1 - y + 2 * (1 - zb)
    weigh((first + 1) % 4)
    pl.semaphore_wait(barrier, 15)
    for r in ((1 - y) + 2, 1 - y, y + 2, y):
        gather(r).start()

    for k, e in enumerate(DISTANCES):
        for s in range(2):
            write(ysend[k].at[s], product(e, (first + 2 * s) % 4))
            ycopy(k, s).start()
            if k == 0:
                weigh((first + 3 - s) % 4)
            elif k == 1 and s == 0:
                weigh(first % 4)

    mask_row = mask_ref[pl.ds(c, 1), :].astype(jnp.float32)
    group_ids = lax.broadcasted_iota(jnp.int32, mask_row.shape, 1)
    level = jnp.sum(jnp.where(group_ids == c, level_ref[...], 0), axis=1, keepdims=True)
    level_ids = lax.broadcasted_iota(jnp.int32, damp_ref.shape, 1)
    damp = jnp.sum(jnp.where(level_ids == level, damp_ref[...], 0.0), axis=1, keepdims=True)

    def masked(q, total):
        mask = jnp.sum(jnp.where(group_ids == 4 * t + q, mask_row, 0.0), axis=1, keepdims=True)
        return total * mask

    def held(e):
        return (t + (rank + e) // 4) % 2 == upper

    def quarter(u, v):
        q = pl.multiple_of(rank * side + v * half_side, half_side)
        return pl.ds(pl.multiple_of(u * half_side, half_side), half_side), pl.ds(q, half_side)

    def over_y(k, e):
        part = product(e, (rank + 2) % 4)
        ycopy(k, 0).wait_recv()
        write(near_send[k], part + read(yrecv[k].at[0]))
        near_copy(k).start()
        part = product(e, rank)
        ycopy(k, 1).wait_recv()
        acc[k][...] = part + read(yrecv[k].at[1])

    def over_near(k, e):
        near_copy(k).wait_recv()
        part = acc[k][...] + read(near_recv[k])

        @pl.when(held(e))
        def _():
            acc[k][...] = part

        @pl.when(jnp.logical_not(held(e)))
        def _():
            write(far_send[k], part)
            far_copy(k).start()

    def over_far(k, e):
        @pl.when(held(e))
        def _():
            far_copy(k).wait_recv()
            total = acc[k][...] + read(far_recv[k])
            if e:
                write(msend[k], total)
                mcopy(k).start()
            q = (rank + e) % 4
            total = masked(q, total)
            if e == 0:
                row_ids = lax.broadcasted_iota(jnp.int32, total.shape, 0)
                col_ids = lax.broadcasted_iota(jnp.int32, total.shape, 1)
                total = total + jnp.where(row_ids == col_ids, damp, 0.0)
            if e != 4:
                out_ref[:, block(q)] = total
            else:
                for u in range(2):
                    rows, cols = quarter(u, (u + upper) % 2)
                    out_ref[rows, cols] = total[u * half_side:(u + 1) * half_side, :]

    def mirror(k, e):
        @pl.when((c + 8 - e) % 8 // 4 == t)
        def _():
            mcopy(k).wait_recv()
            q = (rank + 4 - e) % 4
            total = masked(q, read(mrecv[k]))
            if e != 4:
                out_ref[:, block(q)] = total.T
            else:
                for u in range(2):
                    rows, cols = quarter((u + 1 - upper) % 2, u)
                    out_ref[rows, cols] = total[u * half_side:(u + 1) * half_side, :].T

    steps = (over_y, over_near, over_far)
    for now in range(len(DISTANCES) + 2):
        for lag, step in enumerate(steps):
            if 0 <= now - lag < len(DISTANCES):
                step(now - lag, DISTANCES[now - lag])
    for k, e in enumerate(DISTANCES):
        if e:
            mirror(k, e)

    for r in range(4):
        gather(r).wait_send()
    for k, e in enumerate(DISTANCES):
        for s in range(2):
            ycopy(k, s).wait_send()
        near_copy(k).wait_send()

        @pl.when(jnp.logical_not(held(e)))
        def _():
            far_copy(k).wait_send()

        if e:
            @pl.when(held(e))
            def _():
                mcopy(k).wait_send()


def gram_tiles(sensitivity, cell_weight, pair_mask, level_index, damp_levels):
    groups = pair_mask.shape[0]
    own_rows, cells = sensitivity.shape
    side = 2 * own_rows // groups
    widths = [side // 2 if e == 4 else side for e in DISTANCES]

    def wire(*lead):
        return [pltpu.VMEM(lead + (side + HEAD, width), WIRE) for width in widths]

    dma = pltpu.SemaphoreType.DMA
    return pl.pallas_call(
        functools.partial(gram_kernel, side),
        out_shape=jax.ShapeDtypeStruct((side, own_rows), jnp.float32),
        in_specs=[
            pl.BlockSpec(memory_space=pltpu.VMEM),
            pl.BlockSpec(memory_space=pltpu.VMEM),
            pl.BlockSpec(memory_space=pltpu.VMEM),
            pl.BlockSpec(memory_space=pltpu.VMEM),
            pl.BlockSpec(memory_space=pltpu.HBM),
        ],
        out_specs=pl.BlockSpec(memory_space=pltpu.VMEM),
        scratch_shapes=[
            pltpu.VMEM((2, own_rows, cells), jnp.bfloat16),
            pltpu.VMEM((own_rows, cells), jnp.bfloat16),
            *wire(2), *wire(2), *wire(), *wire(), *wire(), *wire(),
            *[pltpu.VMEM((side, width), jnp.float32) for width in widths],
            *wire(), *wire(),
            dma((4,)), dma((4,)), dma((4,)),
            dma((10,)), dma((10,)), dma((5,)), dma((5,)), dma((5,)), dma((5,)), dma((5,)), dma((5,)),
        ],
        compiler_params=pltpu.CompilerParams(
            collective_id=0, has_side_effects=True, vmem_limit_bytes=60 * 1024 * 1024
        ),
        cost_estimate=pl.CostEstimate(
            flops=2 * 20 * side * side * cells, bytes_accessed=own_rows * cells * 2, transcendentals=0
        ),
    )(cell_weight[None, :], pair_mask, level_index[None, :], damp_levels[None, :], sensitivity)


def plain_sums(sensitivity, cell_weight):
    weighted = (sensitivity.astype(jnp.float32) * cell_weight[None, :]).astype(jnp.bfloat16)
    everyone = lax.all_gather(sensitivity, "tx", axis=0, tiled=True)
    return lax.psum_scatter(contract(everyone, weighted), "cell", scatter_dimension=0, tiled=True)


def local(sensitivity, cell_weight, pair_mask, level_index, damp_levels):
    own_rows = sensitivity.shape[0]
    groups = pair_mask.shape[0]
    total_rows = own_rows * lax.axis_size("tx")
    part_rows = total_rows // lax.axis_size("cell")
    group_rows = total_rows // groups
    tx_pos = lax.axis_index("tx")
    cell_pos = lax.axis_index("cell")
    if lax.axis_size("tx") == 2 and lax.axis_size("cell") == 8 and groups == 8:
        return gram_tiles(sensitivity, cell_weight, pair_mask, level_index, damp_levels)
    summed = plain_sums(sensitivity, cell_weight)
    group = cell_pos * part_rows // group_rows
    col_groups = tx_pos * own_rows // group_rows + jnp.arange(own_rows // group_rows, dtype=jnp.int32)
    mask_row = pair_mask[group][col_groups].astype(jnp.float32)
    damp = damp_levels[level_index[group]]
    row_ids = cell_pos * part_rows + lax.broadcasted_iota(jnp.int32, summed.shape, 0)
    col_ids = tx_pos * own_rows + lax.broadcasted_iota(jnp.int32, summed.shape, 1)
    col_mask = jnp.repeat(mask_row, group_rows)[None, :]
    return summed * col_mask + jnp.where(row_ids == col_ids, damp, 0.0)


def solution(mesh):
    in_specs = (P(("dom", "tx"), "cell"), P(("dom", "cell")), P("dom", None), P("dom"), P("dom"))
    out_specs = P(("dom", "cell"), "tx")
    return jax.shard_map(local, mesh=mesh, in_specs=in_specs, out_specs=out_specs, check_vma=False)
```

```python
import functools

import jax
import jax.numpy as jnp
from jax import lax
from jax.experimental import pallas as pl
from jax.experimental.pallas import tpu as pltpu
from jax.sharding import PartitionSpec as P

MESH = pl.DeviceIdType.MESH
WIRE = jnp.int16
TOP = 32752.0
HEAD = 16
DISTANCES = (1, 2, 3, 4, 0)


def contract(left, right):
    return lax.dot_general(
        left, right, (((1,), (1,)), ((), ())), preferred_element_type=jnp.float32
    )


def write(ref, value):
    side = value.shape[0]
    peak = jnp.maximum(jnp.max(jnp.abs(value), axis=0, keepdims=True), 2.0**-60)
    power = jnp.ceil(jnp.log2(peak))
    ref[pl.ds(0, side), :] = jnp.round(value * (jnp.exp2(-power) * TOP)).astype(jnp.int32).astype(WIRE)
    head = jnp.broadcast_to(power.astype(jnp.int32), (HEAD, value.shape[1]))
    ref[pl.ds(side, HEAD), :] = head.astype(WIRE)


def read(ref):
    side = ref.shape[0] - HEAD
    power = ref[pl.ds(side, HEAD), :].astype(jnp.int32).astype(jnp.float32)[:1, :]
    whole = ref[pl.ds(0, side), :].astype(jnp.int32).astype(jnp.float32)
    return whole * (jnp.exp2(power) * (1.0 / TOP))


def gram_kernel(side, w_ref, mask_ref, level_ref, damp_ref, s_ref, out_ref, sall, wgt, *refs):
    ysend, yrecv, near_send, near_recv, far_send, far_recv, acc, msend, mrecv = (
        refs[n * 5:n * 5 + 5] for n in range(9)
    )
    (load_sem, gsend_sem, grecv_sem, ysend_sem, yrecv_sem, near_send_sem, near_recv_sem,
     far_send_sem, far_recv_sem, msend_sem, mrecv_sem) = refs[45:]
    t = lax.axis_index("tx")
    c = lax.axis_index("cell")
    z, y = c // 2, c % 2
    rank, upper, zb = c % 4, c // 4, z % 2
    half_side = side // 2

    def block(r):
        return pl.ds(pl.multiple_of(r * side, side), side)

    def load(i):
        return pltpu.make_async_copy(
            s_ref.at[pl.ds(i * side, side), :], sall.at[0, pl.ds(i * side, side), :], load_sem.at[i]
        )

    for i in range(4):
        load(i).start()

    barrier = pltpu.get_barrier_semaphore()
    for k in range(1, 16):
        pl.semaphore_signal(
            barrier, inc=1,
            device_id={"tx": (t + k // 8) % 2, "cell": (c + k % 8) % 8},
            device_id_type=MESH,
        )

    def remote(src, dst, send_sem, recv_sem, device):
        return pltpu.make_async_remote_copy(
            src_ref=src, dst_ref=dst, send_sem=send_sem, recv_sem=recv_sem,
            device_id=device, device_id_type=MESH,
        )

    def gather(r):
        return remote(
            s_ref.at[block(r), :], sall.at[1, block(r), :], gsend_sem.at[r], grecv_sem.at[r], {"tx": 1 - t}
        )

    def ycopy(k, s):
        return remote(
            ysend[k].at[s], yrecv[k].at[s], ysend_sem.at[2 * k + s], yrecv_sem.at[2 * k + s],
            {"cell": 2 * z + 1 - y},
        )

    def near_copy(k):
        return remote(
            near_send[k], near_recv[k], near_send_sem.at[k], near_recv_sem.at[k],
            {"cell": 2 * (z + 1 - 2 * zb) + y},
        )

    def far_copy(k):
        return remote(
            far_send[k], far_recv[k], far_send_sem.at[k], far_recv_sem.at[k], {"cell": (c + 4) % 8}
        )

    def mcopy(k):
        return remote(
            msend[k], mrecv[k], msend_sem.at[k], mrecv_sem.at[k],
            {"cell": (c + DISTANCES[k]) % 8, "tx": upper},
        )

    def weigh(i):
        rows = block(i)
        wgt[rows, :] = (sall[0, rows, :].astype(jnp.float32) * w_ref[...]).astype(jnp.bfloat16)

    def product(e, r):
        half, q = (r + e) // 4, (r + e) % 4
        if e:
            @pl.when(r + e == 4)
            def _():
                gather(r).wait_recv()
        if e != 4:
            return contract(sall[half, block(r), :], wgt[block(q), :])
        quarters = []
        for u in range(2):
            v = (u + t + half) % 2
            rows = pl.ds(pl.multiple_of(r * side + u * half_side, half_side), half_side)
            cols = pl.ds(pl.multiple_of(q * side + v * half_side, half_side), half_side)
            quarters.append(contract(sall[half, rows, :], wgt[cols, :]))
        return jnp.concatenate(quarters, axis=0)

    for i in range(4):
        load(i).wait()
    first = 1 - y + 2 * (1 - zb)
    weigh((first + 1) % 4)
    pl.semaphore_wait(barrier, 15)
    for r in ((1 - y) + 2, 1 - y, y + 2, y):
        gather(r).start()

    for k, e in enumerate(DISTANCES):
        for s in range(2):
            write(ysend[k].at[s], product(e, (first + 2 * s) % 4))
            ycopy(k, s).start()
            if k == 0:
                weigh((first + 3 - s) % 4)
            elif k == 1 and s == 0:
                weigh(first % 4)

    mask_row = mask_ref[pl.ds(c, 1), :].astype(jnp.float32)
    group_ids = lax.broadcasted_iota(jnp.int32, mask_row.shape, 1)
    level = jnp.sum(jnp.where(group_ids == c, level_ref[...], 0), axis=1, keepdims=True)
    level_ids = lax.broadcasted_iota(jnp.int32, damp_ref.shape, 1)
    damp = jnp.sum(jnp.where(level_ids == level, damp_ref[...], 0.0), axis=1, keepdims=True)

    def masked(q, total):
        mask = jnp.sum(jnp.where(group_ids == 4 * t + q, mask_row, 0.0), axis=1, keepdims=True)
        return total * mask

    def held(e):
        return (t + (rank + e) // 4) % 2 == upper

    def quarter(u, v):
        q = pl.multiple_of(rank * side + v * half_side, half_side)
        return pl.ds(pl.multiple_of(u * half_side, half_side), half_side), pl.ds(q, half_side)

    def over_y_first(k, e):
        part = product(e, (rank + 2) % 4)
        ycopy(k, 0).wait_recv()
        write(near_send[k], part + read(yrecv[k].at[0]))
        near_copy(k).start()

    def over_y_second(k, e):
        part = product(e, rank)
        ycopy(k, 1).wait_recv()
        acc[k][...] = part + read(yrecv[k].at[1])

    def over_near(k, e):
        near_copy(k).wait_recv()
        part = acc[k][...] + read(near_recv[k])

        @pl.when(held(e))
        def _():
            acc[k][...] = part

        @pl.when(jnp.logical_not(held(e)))
        def _():
            write(far_send[k], part)
            far_copy(k).start()

    def over_far(k, e):
        @pl.when(held(e))
        def _():
            far_copy(k).wait_recv()
            total = acc[k][...] + read(far_recv[k])
            if e:
                write(msend[k], total)
                mcopy(k).start()
            q = (rank + e) % 4
            total = masked(q, total)
            if e == 0:
                row_ids = lax.broadcasted_iota(jnp.int32, total.shape, 0)
                col_ids = lax.broadcasted_iota(jnp.int32, total.shape, 1)
                total = total + jnp.where(row_ids == col_ids, damp, 0.0)
            if e != 4:
                out_ref[:, block(q)] = total
            else:
                for u in range(2):
                    rows, cols = quarter(u, (u + upper) % 2)
                    out_ref[rows, cols] = total[u * half_side:(u + 1) * half_side, :]

    def mirror(k, e):
        @pl.when((c + 8 - e) % 8 // 4 == t)
        def _():
            mcopy(k).wait_recv()
            q = (rank + 4 - e) % 4
            total = masked(q, read(mrecv[k]))
            if e != 4:
                out_ref[:, block(q)] = total.T
            else:
                for u in range(2):
                    rows, cols = quarter((u + 1 - upper) % 2, u)
                    out_ref[rows, cols] = total[u * half_side:(u + 1) * half_side, :].T

    last = len(DISTANCES) - 1
    for k, e in enumerate(DISTANCES):
        over_y_first(k, e)
        if k:
            over_far(k - 1, DISTANCES[k - 1])
        over_y_second(k, e)
        over_near(k, e)
    for k, e in enumerate(DISTANCES):
        if e:
            mirror(k, e)
    over_far(last, DISTANCES[last])

    for r in range(4):
        gather(r).wait_send()
    for k, e in enumerate(DISTANCES):
        for s in range(2):
            ycopy(k, s).wait_send()
        near_copy(k).wait_send()

        @pl.when(jnp.logical_not(held(e)))
        def _():
            far_copy(k).wait_send()

        if e:
            @pl.when(held(e))
            def _():
                mcopy(k).wait_send()


def gram_tiles(sensitivity, cell_weight, pair_mask, level_index, damp_levels):
    groups = pair_mask.shape[0]
    own_rows, cells = sensitivity.shape
    side = 2 * own_rows // groups
    widths = [side // 2 if e == 4 else side for e in DISTANCES]

    def wire(*lead):
        return [pltpu.VMEM(lead + (side + HEAD, width), WIRE) for width in widths]

    dma = pltpu.SemaphoreType.DMA
    return pl.pallas_call(
        functools.partial(gram_kernel, side),
        out_shape=jax.ShapeDtypeStruct((side, own_rows), jnp.float32),
        in_specs=[
            pl.BlockSpec(memory_space=pltpu.VMEM),
            pl.BlockSpec(memory_space=pltpu.VMEM),
            pl.BlockSpec(memory_space=pltpu.VMEM),
            pl.BlockSpec(memory_space=pltpu.VMEM),
            pl.BlockSpec(memory_space=pltpu.HBM),
        ],
        out_specs=pl.BlockSpec(memory_space=pltpu.VMEM),
        scratch_shapes=[
            pltpu.VMEM((2, own_rows, cells), jnp.bfloat16),
            pltpu.VMEM((own_rows, cells), jnp.bfloat16),
            *wire(2), *wire(2), *wire(), *wire(), *wire(), *wire(),
            *[pltpu.VMEM((side, width), jnp.float32) for width in widths],
            *wire(), *wire(),
            dma((4,)), dma((4,)), dma((4,)),
            dma((10,)), dma((10,)), dma((5,)), dma((5,)), dma((5,)), dma((5,)), dma((5,)), dma((5,)),
        ],
        compiler_params=pltpu.CompilerParams(
            collective_id=0, has_side_effects=True, vmem_limit_bytes=60 * 1024 * 1024
        ),
        cost_estimate=pl.CostEstimate(
            flops=2 * 20 * side * side * cells, bytes_accessed=own_rows * cells * 2, transcendentals=0
        ),
    )(cell_weight[None, :], pair_mask, level_index[None, :], damp_levels[None, :], sensitivity)


def plain_sums(sensitivity, cell_weight):
    weighted = (sensitivity.astype(jnp.float32) * cell_weight[None, :]).astype(jnp.bfloat16)
    everyone = lax.all_gather(sensitivity, "tx", axis=0, tiled=True)
    return lax.psum_scatter(contract(everyone, weighted), "cell", scatter_dimension=0, tiled=True)


def local(sensitivity, cell_weight, pair_mask, level_index, damp_levels):
    own_rows = sensitivity.shape[0]
    groups = pair_mask.shape[0]
    total_rows = own_rows * lax.axis_size("tx")
    part_rows = total_rows // lax.axis_size("cell")
    group_rows = total_rows // groups
    tx_pos = lax.axis_index("tx")
    cell_pos = lax.axis_index("cell")
    if lax.axis_size("tx") == 2 and lax.axis_size("cell") == 8 and groups == 8:
        return gram_tiles(sensitivity, cell_weight, pair_mask, level_index, damp_levels)
    summed = plain_sums(sensitivity, cell_weight)
    group = cell_pos * part_rows // group_rows
    col_groups = tx_pos * own_rows // group_rows + jnp.arange(own_rows // group_rows, dtype=jnp.int32)
    mask_row = pair_mask[group][col_groups].astype(jnp.float32)
    damp = damp_levels[level_index[group]]
    row_ids = cell_pos * part_rows + lax.broadcasted_iota(jnp.int32, summed.shape, 0)
    col_ids = tx_pos * own_rows + lax.broadcasted_iota(jnp.int32, summed.shape, 1)
    col_mask = jnp.repeat(mask_row, group_rows)[None, :]
    return summed * col_mask + jnp.where(row_ids == col_ids, damp, 0.0)


def solution(mesh):
    in_specs = (P(("dom", "tx"), "cell"), P(("dom", "cell")), P("dom", None), P("dom"), P("dom"))
    out_specs = P(("dom", "cell"), "tx")
    return jax.shard_map(local, mesh=mesh, in_specs=in_specs, out_specs=out_specs, check_vma=False)
```

```python
import functools

import jax
import jax.numpy as jnp
from jax import lax
from jax.experimental import pallas as pl
from jax.experimental.pallas import tpu as pltpu
from jax.sharding import PartitionSpec as P

MESH = pl.DeviceIdType.MESH
WIRE = jnp.int16
TOP = 32752.0
HEAD = 16
DISTANCES = (1, 2, 3, 4, 0)


def contract(left, right):
    return lax.dot_general(
        left, right, (((1,), (1,)), ((), ())), preferred_element_type=jnp.float32
    )


def write(ref, value):
    side = value.shape[0]
    peak = jnp.maximum(jnp.max(jnp.abs(value), axis=0, keepdims=True), 2.0**-60)
    power = jnp.ceil(jnp.log2(peak))
    ref[pl.ds(0, side), :] = jnp.round(value * (jnp.exp2(-power) * TOP)).astype(jnp.int32).astype(WIRE)
    head = jnp.broadcast_to(power.astype(jnp.int32), (HEAD, value.shape[1]))
    ref[pl.ds(side, HEAD), :] = head.astype(WIRE)


def read(ref):
    side = ref.shape[0] - HEAD
    power = ref[pl.ds(side, HEAD), :].astype(jnp.int32).astype(jnp.float32)[:1, :]
    whole = ref[pl.ds(0, side), :].astype(jnp.int32).astype(jnp.float32)
    return whole * (jnp.exp2(power) * (1.0 / TOP))


def gram_kernel(side, w_ref, mask_ref, level_ref, damp_ref, s_ref, out_ref, sall, wgt, *refs):
    ysend, yrecv, near_send, near_recv, far_send, far_recv, acc, msend, mrecv = (
        refs[n * 5:n * 5 + 5] for n in range(9)
    )
    (load_sem, gsend_sem, grecv_sem, ysend_sem, yrecv_sem, near_send_sem, near_recv_sem,
     far_send_sem, far_recv_sem, msend_sem, mrecv_sem) = refs[45:]
    t = lax.axis_index("tx")
    c = lax.axis_index("cell")
    z, y = c // 2, c % 2
    rank, upper, zb = c % 4, c // 4, z % 2
    half_side = side // 2

    def block(r):
        return pl.ds(pl.multiple_of(r * side, side), side)

    def load(i):
        return pltpu.make_async_copy(
            s_ref.at[pl.ds(i * side, side), :], sall.at[0, pl.ds(i * side, side), :], load_sem.at[i]
        )

    for i in range(4):
        load(i).start()

    barrier = pltpu.get_barrier_semaphore()
    for k in range(1, 16):
        pl.semaphore_signal(
            barrier, inc=1,
            device_id={"tx": (t + k // 8) % 2, "cell": (c + k % 8) % 8},
            device_id_type=MESH,
        )

    def remote(src, dst, send_sem, recv_sem, device):
        return pltpu.make_async_remote_copy(
            src_ref=src, dst_ref=dst, send_sem=send_sem, recv_sem=recv_sem,
            device_id=device, device_id_type=MESH,
        )

    def gather(r):
        return remote(
            s_ref.at[block(r), :], sall.at[1, block(r), :], gsend_sem.at[r], grecv_sem.at[r], {"tx": 1 - t}
        )

    def ycopy(k, s):
        return remote(
            ysend[k].at[s], yrecv[k].at[s], ysend_sem.at[2 * k + s], yrecv_sem.at[2 * k + s],
            {"cell": 2 * z + 1 - y},
        )

    def near_copy(k):
        return remote(
            near_send[k], near_recv[k], near_send_sem.at[k], near_recv_sem.at[k],
            {"cell": 2 * (z + 1 - 2 * zb) + y},
        )

    def far_copy(k):
        return remote(
            far_send[k], far_recv[k], far_send_sem.at[k], far_recv_sem.at[k], {"cell": (c + 4) % 8}
        )

    def mcopy(k):
        return remote(
            msend[k], mrecv[k], msend_sem.at[k], mrecv_sem.at[k],
            {"cell": (c + DISTANCES[k]) % 8, "tx": upper},
        )

    def weigh(i):
        rows = block(i)
        wgt[rows, :] = (sall[0, rows, :].astype(jnp.float32) * w_ref[...]).astype(jnp.bfloat16)

    def product(e, r):
        half, q = (r + e) // 4, (r + e) % 4
        if e:
            @pl.when(r + e == 4)
            def _():
                gather(r).wait_recv()
        if e != 4:
            return contract(sall[half, block(r), :], wgt[block(q), :])
        quarters = []
        for u in range(2):
            v = (u + t + half) % 2
            rows = pl.ds(pl.multiple_of(r * side + u * half_side, half_side), half_side)
            cols = pl.ds(pl.multiple_of(q * side + v * half_side, half_side), half_side)
            quarters.append(contract(sall[half, rows, :], wgt[cols, :]))
        return jnp.concatenate(quarters, axis=0)

    for i in range(4):
        load(i).wait()
    first = 1 - y + 2 * (1 - zb)
    weigh((first + 1) % 4)
    pl.semaphore_wait(barrier, 15)
    for r in ((1 - y) + 2, 1 - y, y + 2, y):
        gather(r).start()

    def send_y(k, e):
        for s in range(2):
            write(ysend[k].at[s], product(e, (first + 2 * s) % 4))
            ycopy(k, s).start()
            if k == 0:
                weigh((first + 3 - s) % 4)
            elif k == 1 and s == 0:
                weigh(first % 4)

    for k in range(2):
        send_y(k, DISTANCES[k])

    mask_row = mask_ref[pl.ds(c, 1), :].astype(jnp.float32)
    group_ids = lax.broadcasted_iota(jnp.int32, mask_row.shape, 1)
    level = jnp.sum(jnp.where(group_ids == c, level_ref[...], 0), axis=1, keepdims=True)
    level_ids = lax.broadcasted_iota(jnp.int32, damp_ref.shape, 1)
    damp = jnp.sum(jnp.where(level_ids == level, damp_ref[...], 0.0), axis=1, keepdims=True)

    def masked(q, total):
        mask = jnp.sum(jnp.where(group_ids == 4 * t + q, mask_row, 0.0), axis=1, keepdims=True)
        return total * mask

    def held(e):
        return (t + (rank + e) // 4) % 2 == upper

    def quarter(u, v):
        q = pl.multiple_of(rank * side + v * half_side, half_side)
        return pl.ds(pl.multiple_of(u * half_side, half_side), half_side), pl.ds(q, half_side)

    def over_y(k, e):
        part = product(e, (rank + 2) % 4)
        ycopy(k, 0).wait_recv()
        write(near_send[k], part + read(yrecv[k].at[0]))
        near_copy(k).start()
        part = product(e, rank)
        ycopy(k, 1).wait_recv()
        acc[k][...] = part + read(yrecv[k].at[1])

    def over_near(k, e):
        near_copy(k).wait_recv()
        part = acc[k][...] + read(near_recv[k])

        @pl.when(held(e))
        def _():
            acc[k][...] = part

        @pl.when(jnp.logical_not(held(e)))
        def _():
            write(far_send[k], part)
            far_copy(k).start()

    def over_far(k, e):
        @pl.when(held(e))
        def _():
            far_copy(k).wait_recv()
            total = acc[k][...] + read(far_recv[k])
            if e:
                write(msend[k], total)
                mcopy(k).start()
            q = (rank + e) % 4
            total = masked(q, total)
            if e == 0:
                row_ids = lax.broadcasted_iota(jnp.int32, total.shape, 0)
                col_ids = lax.broadcasted_iota(jnp.int32, total.shape, 1)
                total = total + jnp.where(row_ids == col_ids, damp, 0.0)
            if e != 4:
                out_ref[:, block(q)] = total
            else:
                for u in range(2):
                    rows, cols = quarter(u, (u + upper) % 2)
                    out_ref[rows, cols] = total[u * half_side:(u + 1) * half_side, :]

    def mirror(k, e):
        @pl.when((c + 8 - e) % 8 // 4 == t)
        def _():
            mcopy(k).wait_recv()
            q = (rank + 4 - e) % 4
            total = masked(q, read(mrecv[k]))
            if e != 4:
                out_ref[:, block(q)] = total.T
            else:
                for u in range(2):
                    rows, cols = quarter((u + 1 - upper) % 2, u)
                    out_ref[rows, cols] = total[u * half_side:(u + 1) * half_side, :].T

    steps = (over_y, over_near, over_far)
    for now in range(len(DISTANCES) + 2):
        for lag, step in enumerate(steps):
            if 0 <= now - lag < len(DISTANCES):
                step(now - lag, DISTANCES[now - lag])
            if lag == 0 and now + 2 < len(DISTANCES):
                send_y(now + 2, DISTANCES[now + 2])
    for k, e in enumerate(DISTANCES):
        if e:
            mirror(k, e)

    for r in range(4):
        gather(r).wait_send()
    for k, e in enumerate(DISTANCES):
        for s in range(2):
            ycopy(k, s).wait_send()
        near_copy(k).wait_send()

        @pl.when(jnp.logical_not(held(e)))
        def _():
            far_copy(k).wait_send()

        if e:
            @pl.when(held(e))
            def _():
                mcopy(k).wait_send()


def gram_tiles(sensitivity, cell_weight, pair_mask, level_index, damp_levels):
    groups = pair_mask.shape[0]
    own_rows, cells = sensitivity.shape
    side = 2 * own_rows // groups
    widths = [side // 2 if e == 4 else side for e in DISTANCES]

    def wire(*lead):
        return [pltpu.VMEM(lead + (side + HEAD, width), WIRE) for width in widths]

    dma = pltpu.SemaphoreType.DMA
    return pl.pallas_call(
        functools.partial(gram_kernel, side),
        out_shape=jax.ShapeDtypeStruct((side, own_rows), jnp.float32),
        in_specs=[
            pl.BlockSpec(memory_space=pltpu.VMEM),
            pl.BlockSpec(memory_space=pltpu.VMEM),
            pl.BlockSpec(memory_space=pltpu.VMEM),
            pl.BlockSpec(memory_space=pltpu.VMEM),
            pl.BlockSpec(memory_space=pltpu.HBM),
        ],
        out_specs=pl.BlockSpec(memory_space=pltpu.VMEM),
        scratch_shapes=[
            pltpu.VMEM((2, own_rows, cells), jnp.bfloat16),
            pltpu.VMEM((own_rows, cells), jnp.bfloat16),
            *wire(2), *wire(2), *wire(), *wire(), *wire(), *wire(),
            *[pltpu.VMEM((side, width), jnp.float32) for width in widths],
            *wire(), *wire(),
            dma((4,)), dma((4,)), dma((4,)),
            dma((10,)), dma((10,)), dma((5,)), dma((5,)), dma((5,)), dma((5,)), dma((5,)), dma((5,)),
        ],
        compiler_params=pltpu.CompilerParams(
            collective_id=0, has_side_effects=True, vmem_limit_bytes=60 * 1024 * 1024
        ),
        cost_estimate=pl.CostEstimate(
            flops=2 * 20 * side * side * cells, bytes_accessed=own_rows * cells * 2, transcendentals=0
        ),
    )(cell_weight[None, :], pair_mask, level_index[None, :], damp_levels[None, :], sensitivity)


def plain_sums(sensitivity, cell_weight):
    weighted = (sensitivity.astype(jnp.float32) * cell_weight[None, :]).astype(jnp.bfloat16)
    everyone = lax.all_gather(sensitivity, "tx", axis=0, tiled=True)
    return lax.psum_scatter(contract(everyone, weighted), "cell", scatter_dimension=0, tiled=True)


def local(sensitivity, cell_weight, pair_mask, level_index, damp_levels):
    own_rows = sensitivity.shape[0]
    groups = pair_mask.shape[0]
    total_rows = own_rows * lax.axis_size("tx")
    part_rows = total_rows // lax.axis_size("cell")
    group_rows = total_rows // groups
    tx_pos = lax.axis_index("tx")
    cell_pos = lax.axis_index("cell")
    if lax.axis_size("tx") == 2 and lax.axis_size("cell") == 8 and groups == 8:
        return gram_tiles(sensitivity, cell_weight, pair_mask, level_index, damp_levels)
    summed = plain_sums(sensitivity, cell_weight)
    group = cell_pos * part_rows // group_rows
    col_groups = tx_pos * own_rows // group_rows + jnp.arange(own_rows // group_rows, dtype=jnp.int32)
    mask_row = pair_mask[group][col_groups].astype(jnp.float32)
    damp = damp_levels[level_index[group]]
    row_ids = cell_pos * part_rows + lax.broadcasted_iota(jnp.int32, summed.shape, 0)
    col_ids = tx_pos * own_rows + lax.broadcasted_iota(jnp.int32, summed.shape, 1)
    col_mask = jnp.repeat(mask_row, group_rows)[None, :]
    return summed * col_mask + jnp.where(row_ids == col_ids, damp, 0.0)


def solution(mesh):
    in_specs = (P(("dom", "tx"), "cell"), P(("dom", "cell")), P("dom", None), P("dom"), P("dom"))
    out_specs = P(("dom", "cell"), "tx")
    return jax.shard_map(local, mesh=mesh, in_specs=in_specs, out_specs=out_specs, check_vma=False)
```
